32 devices in a mesh: tok: 4 (over x, core), hid: 8 (over z, y).
Axes of the slice: x: 2, y: 2, z: 4, core: 2. Of those that a mesh axis runs over, the one named last changes fastest.
Arguments:
- layer_input: bfloat16 [3072, 5120], P(('tok', 'hid')), may hold values from -6 to 6
- output_grad: bfloat16 [3072, 5120], P(('tok', 'hid')), may hold values from -6 to 6
- gate_weight: bfloat16 [5120, 8192], P(None, 'hid'), may hold values from -0.078125 to 0.078125
- up_weight: bfloat16 [5120, 8192], P(None, 'hid'), may hold values from -0.078125 to 0.078125
- down_weight: bfloat16 [8192, 5120], P('hid'), may hold values from -0.0625 to 0.0625
- block_lists: int32 [24, 32], P('tok'), may hold values from 0 to 63, as said below
- block_count: int32 [24], P('tok'), may hold values from 8 to 32, as said below
Outputs:
- input_grad: bfloat16 [3072, 5120], P(('tok', 'hid'))
- gate_grad: bfloat16 [5120, 8192], P('tok', 'hid')
- up_grad: bfloat16 [5120, 8192], P('tok', 'hid')
- down_grad: bfloat16 [8192, 5120], P('hid', 'tok')
The draws below stay inside these ranges and needn't reach their ends.
Inputs may be any that keep to these rules, and one draw needn't show every extreme that they name: Each row of block_lists holds 32 different block numbers; entries past the tile's count are valid block numbers too and are not active. `block_count`: some tile uses all 32 slots and some tile uses 8.
All inputs are finite; a program needn't handle non-finite values.
Results may differ from the reference program's by a relative error of at most 0.015.
Values may be sent and summed in bfloat16 or wider, within the bound.
A program may use at most 192 MiB of HBM per device.

```python
import math
import jax
import jax.numpy as jnp
from jax import lax

D = 5120
FF = 8192
BLOCK = 128
TILE = 128
KMAX = 32
TOKENS = 3072
NTILES = 24
N_HID = 8


def make_lists(key):
    base_key = jax.random.fold_in(key, 31)
    key_favour, key_noise, key_count, key_full, key_short = jax.random.split(base_key, 5)
    overall_block_count = FF // BLOCK
    preference_weight = jax.random.randint(key_favour, (overall_block_count,), 0, 3) * (overall_block_count * 4)
    random_jitter = jax.random.randint(key_noise, (NTILES, overall_block_count), 0, overall_block_count * 8)
    complete_tile = jax.random.randint(key_full, (), 0, NTILES)
    short_tile = (complete_tile + 1 + jax.random.randint(key_short, (), 0, NTILES - 1)) % NTILES
    rows_per_tile = jnp.arange(NTILES)
    block_column_span = jnp.arange(overall_block_count)
    tile_stops = (block_column_span == 0) | (block_column_span == overall_block_count - 1)
    score_boost = jnp.where((rows_per_tile[:, None] == complete_tile) & tile_stops[None, :], overall_block_count * 32, 0)
    predictor_scores = (random_jitter + preference_weight[None, :] + score_boost) * overall_block_count + block_column_span[None, :]
    top_scores, block_ids = jax.lax.top_k(predictor_scores, KMAX)
    counts = jax.random.randint(key_count, (NTILES,), KMAX // 4, KMAX + 1)
    counts = jnp.where(rows_per_tile == complete_tile, KMAX, counts)
    counts = jnp.where(rows_per_tile == short_tile, KMAX // 4, counts)
    return (block_ids.astype(jnp.int32), counts.astype(jnp.int32))


def draw_block_lists(key, part):
    return make_lists(key)[0]


def draw_block_count(key, part):
    return make_lists(key)[1]


def shard_levels(key, shape, pieces, least, largest):
    level = 1.0
    for axis_at, shards_of in pieces:
        steps = jax.random.uniform(jax.random.fold_in(jax.random.fold_in(key, 6), axis_at), (shards_of,), jnp.float32, least / len(pieces), largest / len(pieces))
        level = level * jnp.repeat(jnp.exp(steps), shape[axis_at] // shards_of).reshape((-1,) + (1,) * (len(shape) - 1 - axis_at))
    return level


def scatter_about(stream_key, extent, width, reach, cuts=(), dtype=jnp.bfloat16):
    loudness = shard_levels(stream_key, extent, cuts, -0.22, 0.18) if cuts else 1.0
    array = jax.random.normal(stream_key, extent, jnp.float32) * width * loudness
    return jnp.minimum(jnp.maximum(array, -reach), reach).astype(dtype)


def setup_inputs(seed: int = 0) -> dict:
    seeds = jax.random.split(jax.random.key(seed), 8)
    return {
        "layer_input": scatter_about(seeds[0], (TOKENS, D), 1.0, 6.0, ((0, 32),)),
        "output_grad": scatter_about(seeds[1], (TOKENS, D), 1.0, 6.0, ((0, 32),)),
        "gate_weight": scatter_about(seeds[2], (D, FF), D ** -0.5, 0.078125, ((1, 8),)),
        "up_weight": scatter_about(seeds[3], (D, FF), D ** -0.5, 0.078125, ((1, 8),)),
        "down_weight": scatter_about(seeds[4], (FF, D), FF ** -0.5, 0.0625, ((0, 8),)),
        "block_lists": draw_block_lists(jax.random.fold_in(seeds[7], 71), 0),
        "block_count": draw_block_count(jax.random.fold_in(seeds[7], 71), 0),
    }


def reference(layer_input, output_grad, gate_weight, up_weight, down_weight, block_lists, block_count):
    overall_block_count = FF // BLOCK
    in_list = jnp.arange(KMAX)[None, :] < block_count[:, None]
    hits = (block_lists[:, :, None] == jnp.arange(overall_block_count)[None, None, :]) & in_list[:, :, None]
    tile_mask = jnp.any(hits, axis=1).astype(jnp.float32)
    unit_mask = jnp.repeat(jnp.repeat(tile_mask, TILE, axis=0), BLOCK, axis=1)
    contract_last = (((1,), (1,)), ((), ()))
    contract_first = (((0,), (0,)), ((), ()))
    gate_pre = jnp.dot(layer_input, gate_weight, preferred_element_type=jnp.float32)
    up_pre = jnp.dot(layer_input, up_weight, preferred_element_type=jnp.float32)
    grad_hidden = lax.dot_general(output_grad, down_weight, contract_last, preferred_element_type=jnp.float32)
    sigmoid_g = jax.nn.sigmoid(gate_pre)
    silu_g = gate_pre * sigmoid_g
    hidden = (unit_mask * silu_g * up_pre).astype(jnp.bfloat16)
    grad_gate = (unit_mask * grad_hidden * up_pre * sigmoid_g * (1.0 + gate_pre * (1.0 - sigmoid_g))).astype(jnp.bfloat16)
    grad_up = (unit_mask * grad_hidden * silu_g).astype(jnp.bfloat16)
    group_width = FF // N_HID

    def add_group(shard, total):
        start = (shard * group_width).astype(jnp.int32)
        part_gate = lax.dynamic_slice_in_dim(grad_gate, start, group_width, 1)
        part_up = lax.dynamic_slice_in_dim(grad_up, start, group_width, 1)
        weight_gate = lax.dynamic_slice_in_dim(gate_weight, start, group_width, 1)
        weight_up = lax.dynamic_slice_in_dim(up_weight, start, group_width, 1)
        partial_value = lax.dot_general(part_gate, weight_gate, contract_last, preferred_element_type=jnp.float32)
        partial_value = partial_value + lax.dot_general(part_up, weight_up, contract_last, preferred_element_type=jnp.float32)
        rounded = lax.optimization_barrier(partial_value.astype(jnp.bfloat16))
        return total + rounded.astype(jnp.float32)
    summed = lax.fori_loop(0, N_HID, add_group, jnp.zeros((TOKENS, D), jnp.float32))
    input_grad = summed.astype(jnp.bfloat16)
    scale = 1.0 / math.sqrt(TOKENS)
    gate_grad = (lax.dot_general(layer_input, grad_gate, contract_first, preferred_element_type=jnp.float32) * scale).astype(jnp.bfloat16)
    up_grad = (lax.dot_general(layer_input, grad_up, contract_first, preferred_element_type=jnp.float32) * scale).astype(jnp.bfloat16)
    down_grad = (lax.dot_general(hidden, output_grad, contract_first, preferred_element_type=jnp.float32) * scale).astype(jnp.bfloat16)
    return (input_grad, gate_grad, up_grad, down_grad)
```

```python
import functools
import math

import jax
import jax.numpy as jnp
from jax import lax
from jax.experimental import pallas as pl
from jax.experimental.pallas import tpu as pltpu
from jax.sharding import PartitionSpec as P

BLOCK = 128
TILE = 128
MESH = pl.DeviceIdType.MESH


def partner(t, j, n_tok):
    p = (t + (j // 2) * 2) % n_tok
    if j % 2:
        p = p + 1 - 2 * (p % 2)
    return p


def gather_kernel(n_tok, n_hid, x_ref, g_ref, xf, gf, xc, gc, local_sem, ag_send, ag_recv, col_send, col_recv):
    t = lax.axis_index("tok")
    h = lax.axis_index("hid")
    lines = n_hid // 2
    z, y = h // 2, h % 2
    width = xc.shape[3]
    fulls, cols, mine = (xf, gf), (xc, gc), (x_ref, g_ref)

    barrier = pltpu.get_barrier_semaphore()
    other = z * 2 + 1 - y
    pl.semaphore_signal(barrier, inc=1, device_id=(t, other), device_id_type=MESH)

    @pl.when(z > 0)
    def _():
        pl.semaphore_signal(barrier, inc=1, device_id=(t, h - 2), device_id_type=MESH)

    @pl.when(z < lines - 1)
    def _():
        pl.semaphore_signal(barrier, inc=1, device_id=(t, h + 2), device_id_type=MESH)

    for j in range(1, n_tok):
        pl.semaphore_signal(barrier, inc=1, device_id=(partner(t, j, n_tok), h), device_id_type=MESH)
    pl.semaphore_wait(barrier, n_tok + jnp.where(z > 0, 1, 0) + jnp.where(z < lines - 1, 1, 0))

    def ag(a, src, s, way, dev):
        return pltpu.make_async_remote_copy(
            src_ref=src, dst_ref=fulls[a].at[s], send_sem=ag_send.at[a, way, s], recv_sem=ag_recv.at[a, s],
            device_id=(t, dev), device_id_type=MESH,
        )

    def col(a, src, s, j):
        p = partner(t, j, n_tok)
        return pltpu.make_async_remote_copy(
            src_ref=src.at[:, pl.ds(pl.multiple_of(p * width, 128), width)],
            dst_ref=cols[a].at[j, s],
            send_sem=col_send.at[a, j, s], recv_sem=col_recv.at[a, j, s],
            device_id=(p, h), device_id_type=MESH,
        )

    def own(a, src, s):
        return pltpu.make_async_copy(
            src.at[:, pl.ds(pl.multiple_of(t * width, 128), width)], cols[a].at[0, s], local_sem.at[a, s]
        )

    def full_own(a):
        return pltpu.make_async_copy(mine[a], fulls[a].at[h], local_sem.at[a, n_hid])

    def send_cols(a, src, s):
        for j in range(2, n_tok):
            col(a, src, s, j).start()
        col(a, src, s, 1).start()
        own(a, src, s).start()

    for a in range(2):
        src = mine[a]

        @pl.when(z < lines - 1)
        def _():
            ag(a, src, h, 0, h + 2).start()

        @pl.when(z > 0)
        def _():
            ag(a, src, h, 1, h - 2).start()

        ag(a, src, h, 2, other).start()
    for a in range(2):
        full_own(a).start()
        send_cols(a, mine[a], h)

    for d in range(1, lines):
        for a in range(2):
            @pl.when(z - d >= 0)
            def _():
                s = h - 2 * d
                ag(a, fulls[a].at[s], s, 0, h + 2).wait_recv()

                @pl.when(z < lines - 1)
                def _():
                    ag(a, fulls[a].at[s], s, 0, h + 2).start()

                ag(a, fulls[a].at[s], s, 2, other).start()
                send_cols(a, fulls[a].at[s], s)

            @pl.when(z + d < lines)
            def _():
                s = h + 2 * d
                ag(a, fulls[a].at[s], s, 1, h - 2).wait_recv()

                @pl.when(z > 0)
                def _():
                    ag(a, fulls[a].at[s], s, 1, h - 2).start()

                ag(a, fulls[a].at[s], s, 2, other).start()
                send_cols(a, fulls[a].at[s], s)

        for a in range(2):
            if d == 1:
                ag(a, fulls[a].at[other], other, 2, other).wait_recv()
                send_cols(a, fulls[a].at[other], other)

            @pl.when(z - d >= 0)
            def _():
                s = other - 2 * d
                ag(a, fulls[a].at[s], s, 2, other).wait_recv()
                send_cols(a, fulls[a].at[s], s)

            @pl.when(z + d < lines)
            def _():
                s = other + 2 * d
                ag(a, fulls[a].at[s], s, 2, other).wait_recv()
                send_cols(a, fulls[a].at[s], s)

    for a in range(2):
        full_own(a).wait()
        for zz in range(lines):
            s = zz * 2 + y

            @pl.when(jnp.logical_and(zz <= z, z < lines - 1))
            def _():
                ag(a, fulls[a].at[s], s, 0, h + 2).wait_send()

            @pl.when(jnp.logical_and(zz >= z, z > 0))
            def _():
                ag(a, fulls[a].at[s], s, 1, h - 2).wait_send()

            ag(a, fulls[a].at[s], s, 2, other).wait_send()
        for s in range(n_hid):
            own(a, fulls[a].at[s], s).wait()
            for j in range(1, n_tok):
                col(a, fulls[a].at[s], s, j).wait_send()
                col(a, fulls[a].at[s], s, j).wait_recv()


def gather(layer_input, output_grad, n_tok, n_hid):
    rows, depth = layer_input.shape
    width = depth // n_tok
    full = jax.ShapeDtypeStruct((n_hid, rows, depth), jnp.bfloat16)
    cols = jax.ShapeDtypeStruct((n_tok, n_hid, rows, width), jnp.bfloat16)
    anywhere = pl.BlockSpec(memory_space=pl.ANY)
    return pl.pallas_call(
        functools.partial(gather_kernel, n_tok, n_hid),
        out_shape=(full, full, cols, cols),
        in_specs=[anywhere] * 2,
        out_specs=(anywhere,) * 4,
        scratch_shapes=[
            pltpu.SemaphoreType.DMA((2, n_hid + 1)),
            pltpu.SemaphoreType.DMA((2, 3, n_hid)),
            pltpu.SemaphoreType.DMA((2, n_hid)),
            pltpu.SemaphoreType.DMA((2, n_tok, n_hid)),
            pltpu.SemaphoreType.DMA((2, n_tok, n_hid)),
        ],
        compiler_params=pltpu.CompilerParams(collective_id=0, has_side_effects=True),
        name="gather_rows_and_columns",
    )(layer_input, output_grad)


def unit_grads(gate_pre, up_pre, grad_hidden, unit_mask):
    sigmoid_g = jax.nn.sigmoid(gate_pre)
    silu_g = gate_pre * sigmoid_g
    hidden = (unit_mask * silu_g * up_pre).astype(jnp.bfloat16)
    grad_gate = (
        unit_mask * grad_hidden * up_pre * sigmoid_g * (1.0 + gate_pre * (1.0 - sigmoid_g))
    ).astype(jnp.bfloat16)
    grad_up = (unit_mask * grad_hidden * silu_g).astype(jnp.bfloat16)
    return (hidden, grad_gate, grad_up)


def tile_activity(block_lists, block_count, local_blocks):
    in_list = jnp.arange(block_lists.shape[1])[None, :] < block_count[:, None]
    hits = (block_lists[:, :, None] == local_blocks[None, None, :]) & in_list[:, :, None]
    return jnp.any(hits, axis=1)


def body(layer_input, output_grad, gate_weight, up_weight, down_weight, block_lists, block_count):
    contract_last = (((1,), (1,)), ((), ()))
    contract_first = (((0,), (0,)), ((), ()))
    n_tok, n_hid = lax.axis_size("tok"), lax.axis_size("hid")
    width = gate_weight.shape[1]
    depth = layer_input.shape[1]
    tok_rows = layer_input.shape[0] * n_hid
    blocks_here = width // BLOCK
    local_blocks = lax.axis_index("hid") * blocks_here + jnp.arange(blocks_here, dtype=jnp.int32)
    active = tile_activity(block_lists, block_count, local_blocks)
    inputs_full, grads_full, inputs_cols, grads_cols = gather(layer_input, output_grad, n_tok, n_hid)
    inputs_full = inputs_full.reshape(tok_rows, depth)
    grads_full = grads_full.reshape(tok_rows, depth)
    inputs_cols = inputs_cols.reshape(n_tok * tok_rows, depth // n_tok)
    grads_cols = grads_cols.reshape(n_tok * tok_rows, depth // n_tok)
    tiles_here = tok_rows // TILE
    unit_mask = jnp.broadcast_to(
        active.astype(jnp.float32)[:, None, :, None], (tiles_here, TILE, blocks_here, BLOCK)
    ).reshape(tok_rows, width)
    gate_pre = jnp.dot(inputs_full, gate_weight, preferred_element_type=jnp.float32)
    up_pre = jnp.dot(inputs_full, up_weight, preferred_element_type=jnp.float32)
    grad_hidden = lax.dot_general(
        grads_full, down_weight, contract_last, preferred_element_type=jnp.float32
    )
    acts = unit_grads(gate_pre, up_pre, grad_hidden, unit_mask)
    _, grad_gate, grad_up = acts
    total = lax.dot_general(
        grad_gate, gate_weight, contract_last, preferred_element_type=jnp.float32
    )
    input_grad = lax.psum_scatter(
        (
            total
            + lax.dot_general(grad_up, up_weight, contract_last, preferred_element_type=jnp.float32)
        ).astype(jnp.bfloat16),
        "hid",
        scatter_dimension=0,
        tiled=True,
    )
    over_core = [(i, i + 1 - 2 * (i % 2)) for i in range(n_tok)]
    slots = [[], [], []]
    for k in range(n_tok // 2):
        for i, arr in enumerate(acts):
            if k:
                arr = lax.ppermute(arr, "tok", [(d, (d + 2 * k) % n_tok) for d in range(n_tok)])
            slots[i] += [arr, lax.ppermute(arr, "tok", over_core)]
    scale = 1.0 / math.sqrt(tok_rows * n_tok)
    near = 2 * tok_rows

    def weight_sum(columns, parts):
        first = lax.dot_general(
            columns[:near], jnp.concatenate(parts[:2]), contract_first, preferred_element_type=jnp.float32
        )
        rest = lax.dot_general(
            columns[near:], jnp.concatenate(parts[2:]), contract_first, preferred_element_type=jnp.float32
        )
        return (first + rest) * scale

    gate_grad = weight_sum(inputs_cols, slots[1]).astype(jnp.bfloat16)
    up_grad = weight_sum(inputs_cols, slots[2]).astype(jnp.bfloat16)
    down_grad = weight_sum(grads_cols, slots[0]).T.astype(jnp.bfloat16)
    return (input_grad, gate_grad, up_grad, down_grad)


def solution(mesh):
    in_specs = (
        P(("tok", "hid"), None),
        P(("tok", "hid"), None),
        P(None, "hid"),
        P(None, "hid"),
        P("hid", None),
        P("tok", None),
        P("tok"),
    )
    out_specs = (P(("tok", "hid"), None), P("tok", "hid"), P("tok", "hid"), P("hid", "tok"))
    return jax.shard_map(body, mesh=mesh, in_specs=in_specs, out_specs=out_specs, check_vma=False)
```

```python
import functools
import math

import jax
import jax.numpy as jnp
import numpy as np
from jax import lax
from jax.experimental import pallas as pl
from jax.experimental.pallas import tpu as pltpu
from jax.sharding import PartitionSpec as P

BLOCK = 128
TILE = 128
MESH = pl.DeviceIdType.MESH


def partner(t, j, n_tok):
    p = (t + (j // 2) * 2) % n_tok
    if j % 2:
        p = p + 1 - 2 * (p % 2)
    return p


def gather_kernel(n_tok, n_hid, *refs):
    x_ref, g_ref = refs[:2]
    xf, gf, xc, gc, local_sem, ag_send, ag_recv, col_send, col_recv = refs[-9:]
    t = lax.axis_index("tok")
    h = lax.axis_index("hid")
    lines = n_hid // 2
    z, y = h // 2, h % 2
    width = xc.shape[3]
    fulls, cols, mine = (xf, gf), (xc, gc), (x_ref, g_ref)

    barrier = pltpu.get_barrier_semaphore()
    other = z * 2 + 1 - y
    pl.semaphore_signal(barrier, inc=1, device_id=(t, other), device_id_type=MESH)

    @pl.when(z > 0)
    def _():
        pl.semaphore_signal(barrier, inc=1, device_id=(t, h - 2), device_id_type=MESH)

    @pl.when(z < lines - 1)
    def _():
        pl.semaphore_signal(barrier, inc=1, device_id=(t, h + 2), device_id_type=MESH)

    for j in range(1, n_tok):
        pl.semaphore_signal(barrier, inc=1, device_id=(partner(t, j, n_tok), h), device_id_type=MESH)
    pl.semaphore_wait(barrier, n_tok + jnp.where(z > 0, 1, 0) + jnp.where(z < lines - 1, 1, 0))

    def ag(a, src, s, way, dev):
        return pltpu.make_async_remote_copy(
            src_ref=src, dst_ref=fulls[a].at[s], send_sem=ag_send.at[a, way, s], recv_sem=ag_recv.at[a, s],
            device_id=(t, dev), device_id_type=MESH,
        )

    def col(a, src, s, j):
        p = partner(t, j, n_tok)
        return pltpu.make_async_remote_copy(
            src_ref=src.at[:, pl.ds(pl.multiple_of(p * width, 128), width)],
            dst_ref=cols[a].at[j, s],
            send_sem=col_send.at[a, j, s], recv_sem=col_recv.at[a, j, s],
            device_id=(p, h), device_id_type=MESH,
        )

    def own(a, src, s):
        return pltpu.make_async_copy(
            src.at[:, pl.ds(pl.multiple_of(t * width, 128), width)], cols[a].at[0, s], local_sem.at[a, s]
        )

    def full_own(a):
        return pltpu.make_async_copy(mine[a], fulls[a].at[h], local_sem.at[a, n_hid])

    def send_cols(a, src, s):
        for j in range(2, n_tok):
            col(a, src, s, j).start()
        col(a, src, s, 1).start()
        own(a, src, s).start()

    for a in range(2):
        src = mine[a]

        @pl.when(z < lines - 1)
        def _():
            ag(a, src, h, 0, h + 2).start()

        @pl.when(z > 0)
        def _():
            ag(a, src, h, 1, h - 2).start()

        ag(a, src, h, 2, other).start()
    for a in range(2):
        full_own(a).start()
        send_cols(a, mine[a], h)

    for d in range(1, lines):
        for a in range(2):
            @pl.when(z - d >= 0)
            def _():
                s = h - 2 * d
                ag(a, fulls[a].at[s], s, 0, h + 2).wait_recv()

                @pl.when(z < lines - 1)
                def _():
                    ag(a, fulls[a].at[s], s, 0, h + 2).start()

                ag(a, fulls[a].at[s], s, 2, other).start()
                send_cols(a, fulls[a].at[s], s)

            @pl.when(z + d < lines)
            def _():
                s = h + 2 * d
                ag(a, fulls[a].at[s], s, 1, h - 2).wait_recv()

                @pl.when(z > 0)
                def _():
                    ag(a, fulls[a].at[s], s, 1, h - 2).start()

                ag(a, fulls[a].at[s], s, 2, other).start()
                send_cols(a, fulls[a].at[s], s)

        for a in range(2):
            if d == 1:
                ag(a, fulls[a].at[other], other, 2, other).wait_recv()
                send_cols(a, fulls[a].at[other], other)

            @pl.when(z - d >= 0)
            def _():
                s = other - 2 * d
                ag(a, fulls[a].at[s], s, 2, other).wait_recv()
                send_cols(a, fulls[a].at[s], s)

            @pl.when(z + d < lines)
            def _():
                s = other + 2 * d
                ag(a, fulls[a].at[s], s, 2, other).wait_recv()
                send_cols(a, fulls[a].at[s], s)

    for a in range(2):
        full_own(a).wait()
        for zz in range(lines):
            s = zz * 2 + y

            @pl.when(jnp.logical_and(zz <= z, z < lines - 1))
            def _():
                ag(a, fulls[a].at[s], s, 0, h + 2).wait_send()

            @pl.when(jnp.logical_and(zz >= z, z > 0))
            def _():
                ag(a, fulls[a].at[s], s, 1, h - 2).wait_send()

            ag(a, fulls[a].at[s], s, 2, other).wait_send()
        for s in range(n_hid):
            own(a, fulls[a].at[s], s).wait()
            for j in range(1, n_tok):
                col(a, fulls[a].at[s], s, j).wait_send()
                col(a, fulls[a].at[s], s, j).wait_recv()


def gather(layer_input, output_grad, n_tok, n_hid, call, after):
    rows, depth = layer_input.shape
    width = depth // n_tok
    full = jax.ShapeDtypeStruct((n_hid, rows, depth), jnp.bfloat16)
    cols = jax.ShapeDtypeStruct((n_tok, n_hid, rows, width), jnp.bfloat16)
    anywhere = pl.BlockSpec(memory_space=pl.ANY)
    return pl.pallas_call(
        functools.partial(gather_kernel, n_tok, n_hid),
        out_shape=(full, full, cols, cols),
        in_specs=[anywhere] * (2 + len(after)),
        out_specs=(anywhere,) * 4,
        scratch_shapes=[
            pltpu.SemaphoreType.DMA((2, n_hid + 1)),
            pltpu.SemaphoreType.DMA((2, 3, n_hid)),
            pltpu.SemaphoreType.DMA((2, n_hid)),
            pltpu.SemaphoreType.DMA((2, n_tok, n_hid)),
            pltpu.SemaphoreType.DMA((2, n_tok, n_hid)),
        ],
        compiler_params=pltpu.CompilerParams(collective_id=call, has_side_effects=True),
        cost_estimate=pl.CostEstimate(flops=0, bytes_accessed=rows * n_hid * depth * 40, transcendentals=0),
        name="gather_rows_and_columns_%d" % call,
    )(layer_input, output_grad, *after)


def hold_until(values, after):
    anywhere = pl.BlockSpec(memory_space=pl.ANY)
    return pl.pallas_call(
        lambda *refs: None,
        out_shape=[jax.ShapeDtypeStruct(v.shape, v.dtype) for v in values],
        in_specs=[anywhere] * (len(values) + len(after)),
        out_specs=[anywhere] * len(values),
        input_output_aliases={i: i for i in range(len(values))},
        name="hold_until",
    )(*values, *after)


def unit_grads(gate_pre, up_pre, grad_hidden, unit_mask):
    sigmoid_g = jax.nn.sigmoid(gate_pre)
    silu_g = gate_pre * sigmoid_g
    hidden = (unit_mask * silu_g * up_pre).astype(jnp.bfloat16)
    grad_gate = (
        unit_mask * grad_hidden * up_pre * sigmoid_g * (1.0 + gate_pre * (1.0 - sigmoid_g))
    ).astype(jnp.bfloat16)
    grad_up = (unit_mask * grad_hidden * silu_g).astype(jnp.bfloat16)
    return (hidden, grad_gate, grad_up)


def tile_activity(block_lists, block_count, local_blocks):
    in_list = jnp.arange(block_lists.shape[1])[None, :] < block_count[:, None]
    hits = (block_lists[:, :, None] == local_blocks[None, None, :]) & in_list[:, :, None]
    return jnp.any(hits, axis=1)


def body(layer_input, output_grad, gate_weight, up_weight, down_weight, block_lists, block_count):
    contract_last = (((1,), (1,)), ((), ()))
    contract_first = (((0,), (0,)), ((), ()))
    n_tok, n_hid = lax.axis_size("tok"), lax.axis_size("hid")
    width = gate_weight.shape[1]
    rows, depth = layer_input.shape
    tok_rows = rows * n_hid
    blocks_here = width // BLOCK
    local_blocks = lax.axis_index("hid") * blocks_here + jnp.arange(blocks_here, dtype=jnp.int32)
    active = tile_activity(block_lists, block_count, local_blocks).astype(jnp.float32)
    over_core = [(i, i + 1 - 2 * (i % 2)) for i in range(n_tok)]
    scale = 1.0 / math.sqrt(tok_rows * n_tok)

    def front(x, g, first_row, call, start_after=(), use_after=()):
        n = x.shape[0]
        x_full, g_full, x_cols, g_cols = gather(x, g, n_tok, n_hid, call, start_after)
        if use_after:
            x_full, g_full = hold_until((x_full, g_full), use_after)
        x_full, g_full = x_full.reshape(n * n_hid, depth), g_full.reshape(n * n_hid, depth)
        tiles = (np.arange(n_hid)[:, None] * rows + first_row + np.arange(n)[None, :]).reshape(-1) // TILE
        pick = jnp.asarray(tiles)[:, None] == jnp.arange(active.shape[0])[None, :]
        row_active = jnp.dot(pick.astype(jnp.float32), active)
        unit_mask = jnp.broadcast_to(row_active[:, :, None], (n * n_hid, blocks_here, BLOCK)).reshape(-1, width)
        gate_pre = jnp.dot(x_full, gate_weight, preferred_element_type=jnp.float32)
        up_pre = jnp.dot(x_full, up_weight, preferred_element_type=jnp.float32)
        grad_hidden = lax.dot_general(g_full, down_weight, contract_last, preferred_element_type=jnp.float32)
        acts = unit_grads(gate_pre, up_pre, grad_hidden, unit_mask)
        return acts, x_cols.reshape(-1, x_cols.shape[-1]), g_cols.reshape(-1, g_cols.shape[-1])

    def input_partial(acts):
        _, grad_gate, grad_up = acts
        total = lax.dot_general(grad_gate, gate_weight, contract_last, preferred_element_type=jnp.float32)
        return (
            total + lax.dot_general(grad_up, up_weight, contract_last, preferred_element_type=jnp.float32)
        ).astype(jnp.bfloat16)

    def cross(acts):
        far = [[(d, (d + 2 * k) % n_tok) for d in range(n_tok)] for k in range(1, n_tok // 2)]
        return [[lax.ppermute(arr, "tok", perm) for perm in far] for arr in acts]

    def spread(acts, crossed):
        slots = []
        for arr, others in zip(acts, crossed):
            parts = []
            for one in [arr] + others:
                parts += [one, lax.ppermute(one, "tok", over_core)]
            slots.append(jnp.concatenate(parts))
        return slots

    def scatter(partial):
        return lax.psum_scatter(partial, "hid", scatter_dimension=0, tiled=True)

    cut = rows * 2 // 3
    acts0, x_cols0, g_cols0 = front(layer_input[:cut], output_grad[:cut], 0, 0)
    crossed0 = cross(acts0)
    partial0 = input_partial(acts0)
    input_grad0 = scatter(partial0)
    acts1, x_cols1, g_cols1 = front(
        layer_input[cut:], output_grad[cut:], cut, 1, (partial0,), (input_grad0, *sum(crossed0, []))
    )
    crossed1 = cross(acts1)
    input_grad = jnp.concatenate([input_grad0, scatter(input_partial(acts1))])
    all0, all1 = spread(acts0, crossed0), spread(acts1, crossed1)

    def weight_sum(cols0, cols1, i):
        return (
            lax.dot_general(cols0, all0[i], contract_first, preferred_element_type=jnp.float32)
            + lax.dot_general(cols1, all1[i], contract_first, preferred_element_type=jnp.float32)
        ) * scale

    gate_grad = weight_sum(x_cols0, x_cols1, 1).astype(jnp.bfloat16)
    up_grad = weight_sum(x_cols0, x_cols1, 2).astype(jnp.bfloat16)
    down_grad = weight_sum(g_cols0, g_cols1, 0).T.astype(jnp.bfloat16)
    return (input_grad, gate_grad, up_grad, down_grad)


def solution(mesh):
    in_specs = (
        P(("tok", "hid"), None),
        P(("tok", "hid"), None),
        P(None, "hid"),
        P(None, "hid"),
        P("hid", None),
        P("tok", None),
        P("tok"),
    )
    out_specs = (P(("tok", "hid"), None), P("tok", "hid"), P("tok", "hid"), P("hid", "tok"))
    return jax.shard_map(body, mesh=mesh, in_specs=in_specs, out_specs=out_specs, check_vma=False)
```

```python
import functools
import math

import jax
import jax.numpy as jnp
from jax import lax
from jax.experimental import pallas as pl
from jax.experimental.pallas import tpu as pltpu
from jax.sharding import PartitionSpec as P

BLOCK = 128
TILE = 128
MESH = pl.DeviceIdType.MESH


def partner(t, j, n_tok):
    p = (t + (j // 2) * 2) % n_tok
    if j % 2:
        p = p + 1 - 2 * (p % 2)
    return p


def gather_kernel(n_tok, n_hid, x_ref, g_ref, xf, gf, xc, gc, local_sem, ag_send, ag_recv, col_send, col_recv):
    t = lax.axis_index("tok")
    h = lax.axis_index("hid")
    lines = n_hid // 2
    z, y = h // 2, h % 2
    width = xc.shape[3]
    fulls, cols, mine = (xf, gf), (xc, gc), (x_ref, g_ref)

    barrier = pltpu.get_barrier_semaphore()
    other = z * 2 + 1 - y
    pl.semaphore_signal(barrier, inc=1, device_id=(t, other), device_id_type=MESH)

    @pl.when(z > 0)
    def _():
        pl.semaphore_signal(barrier, inc=1, device_id=(t, h - 2), device_id_type=MESH)

    @pl.when(z < lines - 1)
    def _():
        pl.semaphore_signal(barrier, inc=1, device_id=(t, h + 2), device_id_type=MESH)

    for j in range(1, n_tok):
        pl.semaphore_signal(barrier, inc=1, device_id=(partner(t, j, n_tok), h), device_id_type=MESH)
    pl.semaphore_wait(barrier, n_tok + jnp.where(z > 0, 1, 0) + jnp.where(z < lines - 1, 1, 0))

    rows = x_ref.shape[0]
    late = rows // 6 if rows % 96 == 0 else 0
    spans = ((0, rows - late), (rows - late, late)) if late else ((0, rows),)
    both = tuple(range(len(spans)))

    def ag(a, src, s, way, dev, part=0):
        lo, n = spans[part]
        return pltpu.make_async_remote_copy(
            src_ref=src.at[pl.ds(lo, n)], dst_ref=fulls[a].at[s, pl.ds(lo, n)],
            send_sem=ag_send.at[a, part, way, s], recv_sem=ag_recv.at[a, part, s],
            device_id=(t, dev), device_id_type=MESH,
        )

    def col(a, src, s, j):
        p = partner(t, j, n_tok)
        return pltpu.make_async_remote_copy(
            src_ref=src.at[:, pl.ds(pl.multiple_of(p * width, 128), width)],
            dst_ref=cols[a].at[j, s],
            send_sem=col_send.at[a, j, s], recv_sem=col_recv.at[a, j, s],
            device_id=(p, h), device_id_type=MESH,
        )

    def own(a, src, s):
        return pltpu.make_async_copy(
            src.at[:, pl.ds(pl.multiple_of(t * width, 128), width)], cols[a].at[0, s], local_sem.at[a, s]
        )

    def full_own(a):
        return pltpu.make_async_copy(mine[a], fulls[a].at[h], local_sem.at[a, n_hid])

    def send_cols(a, src, s):
        for j in range(2, n_tok):
            col(a, src, s, j).start()
        col(a, src, s, 1).start()
        own(a, src, s).start()

    for a in range(2):
        src = mine[a]

        @pl.when(z < lines - 1)
        def _():
            for part in both:
                ag(a, src, h, 0, h + 2, part).start()

        @pl.when(z > 0)
        def _():
            for part in both:
                ag(a, src, h, 1, h - 2, part).start()

        for part in both[::-1]:
            ag(a, src, h, 2, other, part).start()
    for a in range(2):
        full_own(a).start()
        send_cols(a, mine[a], h)

    def pass_on(a, s, way, part):
        src = fulls[a].at[s]
        if way == 0:
            @pl.when(z < lines - 1)
            def _():
                ag(a, src, s, 0, h + 2, part).start()
        else:
            @pl.when(z > 0)
            def _():
                ag(a, src, s, 1, h - 2, part).start()

    if late:
        for a in range(2):
            ag(a, fulls[a].at[other], other, 2, other, 1).wait_recv()
            pass_on(a, other, 0, 1)
            pass_on(a, other, 1, 1)

    def own_line(a, s, way):
        for part in both:
            ag(a, fulls[a].at[s], s, way, other, part).wait_recv()
            pass_on(a, s, way, part)
        ag(a, fulls[a].at[s], s, 2, other).start()
        send_cols(a, fulls[a].at[s], s)

    def other_line(a, s, way):
        if late:
            ag(a, fulls[a].at[s], s, way, other, 1).wait_recv()
            pass_on(a, s, way, 1)
        ag(a, fulls[a].at[s], s, 2, other).wait_recv()
        send_cols(a, fulls[a].at[s], s)

    for d in range(1, lines):
        for a in range(2):
            @pl.when(z - d >= 0)
            def _():
                own_line(a, h - 2 * d, 0)

            @pl.when(z + d < lines)
            def _():
                own_line(a, h + 2 * d, 1)

        for a in range(2):
            if d == 1:
                ag(a, fulls[a].at[other], other, 2, other).wait_recv()
                send_cols(a, fulls[a].at[other], other)

            @pl.when(z - d >= 0)
            def _():
                other_line(a, other - 2 * d, 0)

            @pl.when(z + d < lines)
            def _():
                other_line(a, other + 2 * d, 1)

    for a in range(2):
        full_own(a).wait()
        for zz in range(lines):
            s = zz * 2 + y
            crossing = zz * 2 + 1 - y

            @pl.when(jnp.logical_and(zz <= z, z < lines - 1))
            def _():
                for part in both:
                    ag(a, fulls[a].at[s], s, 0, h + 2, part).wait_send()
                if late:
                    ag(a, fulls[a].at[crossing], crossing, 0, h + 2, 1).wait_send()

            @pl.when(jnp.logical_and(zz >= z, z > 0))
            def _():
                for part in both:
                    ag(a, fulls[a].at[s], s, 1, h - 2, part).wait_send()
                if late:
                    ag(a, fulls[a].at[crossing], crossing, 1, h - 2, 1).wait_send()

            ag(a, fulls[a].at[s], s, 2, other).wait_send()
        if late:
            ag(a, fulls[a].at[h], h, 2, other, 1).wait_send()
        for s in range(n_hid):
            own(a, fulls[a].at[s], s).wait()
            for j in range(1, n_tok):
                col(a, fulls[a].at[s], s, j).wait_send()
                col(a, fulls[a].at[s], s, j).wait_recv()


def gather(layer_input, output_grad, n_tok, n_hid):
    rows, depth = layer_input.shape
    width = depth // n_tok
    full = jax.ShapeDtypeStruct((n_hid, rows, depth), jnp.bfloat16)
    cols = jax.ShapeDtypeStruct((n_tok, n_hid, rows, width), jnp.bfloat16)
    anywhere = pl.BlockSpec(memory_space=pl.ANY)
    return pl.pallas_call(
        functools.partial(gather_kernel, n_tok, n_hid),
        out_shape=(full, full, cols, cols),
        in_specs=[anywhere] * 2,
        out_specs=(anywhere,) * 4,
        scratch_shapes=[
            pltpu.SemaphoreType.DMA((2, n_hid + 1)),
            pltpu.SemaphoreType.DMA((2, 2, 3, n_hid)),
            pltpu.SemaphoreType.DMA((2, 2, n_hid)),
            pltpu.SemaphoreType.DMA((2, n_tok, n_hid)),
            pltpu.SemaphoreType.DMA((2, n_tok, n_hid)),
        ],
        compiler_params=pltpu.CompilerParams(collective_id=0, has_side_effects=True),
        name="gather_rows_and_columns",
    )(layer_input, output_grad)


def unit_grads(gate_pre, up_pre, grad_hidden, unit_mask):
    sigmoid_g = jax.nn.sigmoid(gate_pre)
    silu_g = gate_pre * sigmoid_g
    hidden = (unit_mask * silu_g * up_pre).astype(jnp.bfloat16)
    grad_gate = (
        unit_mask * grad_hidden * up_pre * sigmoid_g * (1.0 + gate_pre * (1.0 - sigmoid_g))
    ).astype(jnp.bfloat16)
    grad_up = (unit_mask * grad_hidden * silu_g).astype(jnp.bfloat16)
    return (hidden, grad_gate, grad_up)


def tile_activity(block_lists, block_count, local_blocks):
    in_list = jnp.arange(block_lists.shape[1])[None, :] < block_count[:, None]
    hits = (block_lists[:, :, None] == local_blocks[None, None, :]) & in_list[:, :, None]
    return jnp.any(hits, axis=1)


def body(layer_input, output_grad, gate_weight, up_weight, down_weight, block_lists, block_count):
    contract_last = (((1,), (1,)), ((), ()))
    contract_first = (((0,), (0,)), ((), ()))
    n_tok, n_hid = lax.axis_size("tok"), lax.axis_size("hid")
    width = gate_weight.shape[1]
    depth = layer_input.shape[1]
    tok_rows = layer_input.shape[0] * n_hid
    blocks_here = width // BLOCK
    local_blocks = lax.axis_index("hid") * blocks_here + jnp.arange(blocks_here, dtype=jnp.int32)
    active = tile_activity(block_lists, block_count, local_blocks)
    inputs_full, grads_full, inputs_cols, grads_cols = gather(layer_input, output_grad, n_tok, n_hid)
    inputs_full = inputs_full.reshape(tok_rows, depth)
    grads_full = grads_full.reshape(tok_rows, depth)
    inputs_cols = inputs_cols.reshape(n_tok * tok_rows, depth // n_tok)
    grads_cols = grads_cols.reshape(n_tok * tok_rows, depth // n_tok)
    tiles_here = tok_rows // TILE
    unit_mask = jnp.broadcast_to(
        active.astype(jnp.float32)[:, None, :, None], (tiles_here, TILE, blocks_here, BLOCK)
    ).reshape(tok_rows, width)
    gate_pre = jnp.dot(inputs_full, gate_weight, preferred_element_type=jnp.float32)
    up_pre = jnp.dot(inputs_full, up_weight, preferred_element_type=jnp.float32)
    grad_hidden = lax.dot_general(
        grads_full, down_weight, contract_last, preferred_element_type=jnp.float32
    )
    acts = unit_grads(gate_pre, up_pre, grad_hidden, unit_mask)
    _, grad_gate, grad_up = acts
    total = lax.dot_general(
        grad_gate, gate_weight, contract_last, preferred_element_type=jnp.float32
    )
    input_grad = lax.psum_scatter(
        (
            total
            + lax.dot_general(grad_up, up_weight, contract_last, preferred_element_type=jnp.float32)
        ).astype(jnp.bfloat16),
        "hid",
        scatter_dimension=0,
        tiled=True,
    )
    over_core = [(i, i + 1 - 2 * (i % 2)) for i in range(n_tok)]
    slots = [[], [], []]
    for k in range(n_tok // 2):
        for i, arr in enumerate(acts):
            if k:
                arr = lax.ppermute(arr, "tok", [(d, (d + 2 * k) % n_tok) for d in range(n_tok)])
            slots[i] += [arr, lax.ppermute(arr, "tok", over_core)]
    scale = 1.0 / math.sqrt(tok_rows * n_tok)
    near = 2 * tok_rows

    def weight_sum(columns, parts):
        first = lax.dot_general(
            columns[:near], jnp.concatenate(parts[:2]), contract_first, preferred_element_type=jnp.float32
        )
        rest = lax.dot_general(
            columns[near:], jnp.concatenate(parts[2:]), contract_first, preferred_element_type=jnp.float32
        )
        return (first + rest) * scale

    gate_grad = weight_sum(inputs_cols, slots[1]).astype(jnp.bfloat16)
    up_grad = weight_sum(inputs_cols, slots[2]).astype(jnp.bfloat16)
    down_grad = weight_sum(grads_cols, slots[0]).T.astype(jnp.bfloat16)
    return (input_grad, gate_grad, up_grad, down_grad)


def solution(mesh):
    in_specs = (
        P(("tok", "hid"), None),
        P(("tok", "hid"), None),
        P(None, "hid"),
        P(None, "hid"),
        P("hid", None),
        P("tok", None),
        P("tok"),
    )
    out_specs = (P(("tok", "hid"), None), P("tok", "hid"), P("tok", "hid"), P("hid", "tok"))
    return jax.shard_map(body, mesh=mesh, in_specs=in_specs, out_specs=out_specs, check_vma=False)
```
